512 devices in a mesh: gx: 32 (over z_hi, y, core), gy: 16 (over z_lo, x).
Axes of the slice: x: 4, y: 8, z: 8 (z_hi: 2, z_lo: 4; z = z_hi * 4 + z_lo), core: 2. Of those that a mesh axis runs over, the one named last changes fastest.
Arguments:
- offsets: bfloat16 [642, 3, 65536], P(None, None, ('gx', 'gy')), may hold values from -6 to 6
- metric: bfloat16 [642, 65536], P(None, ('gx', 'gy')), may hold values from 0.29882812 to 3
- centers: float32 [3, 65536], P(None, ('gx', 'gy')), may hold values from -6 to 6
- lap_matrix: bfloat16 [642, 642], replicated, may hold values from -0.25 to 0.25
- bend_matrix: bfloat16 [642, 642], replicated, may hold values from -0.25 to 0.25
- mig_slots: int32 [512, 8, 4], P(('gx', 'gy')), may hold values from 0 to 127, as said below
- contact_ids: int32 [512, 8, 4], P(('gx', 'gy')), may hold values from 0 to 767
- contact_local: int32 [512, 8, 4], P(('gx', 'gy')), may hold values from 0 to 127
- contact_count: int32 [512, 8], P(('gx', 'gy')), may hold values from 1 to 4, as said below
Outputs:
- new_offsets: bfloat16 [642, 3, 65536], P(None, None, ('gx', 'gy'))
- new_metric: bfloat16 [642, 65536], P(None, ('gx', 'gy'))
- new_centers: float32 [3, 65536], P(None, ('gx', 'gy'))
The draws below stay inside these ranges and needn't reach their ends.
Inputs may be any that keep to these rules, and one draw needn't show every extreme that they name: `mig_slots`: within one tile the slots named over all 8 directions are distinct. `contact_count`: in every draw some tile has exactly 4 live entries toward some neighbour. `contact_ids`: entries at or past the count are unused.
All inputs are finite; a program needn't handle non-finite values.
Results may differ from the reference program's by a relative error of at most 0.0032.
Values sent between devices are 32-bit elements; how exact they have to be, the bound alone decides.
A program may use at most 64 MiB of HBM per device.

```python
import math
import jax
import jax.numpy as jnp
from jax import lax

V = 642
NBLK = 6
VB = 107
CELLS_DEV = 128
MIG = 4
CAP = 4
TILES = 512
CELLS = 65536
N_GX = 32
N_GY = 16


def draw_mig_slots(key, part):
    keys = jax.random.split(key, TILES)

    def one_tile(tile_key):
        return jax.random.permutation(tile_key, CELLS_DEV)[:8 * MIG].reshape(8, MIG)
    return jax.vmap(one_tile)(keys).astype(jnp.int32)


def draw_contact_count(key, part):
    key_dense, key_low, key_high, key_peak, key_dir = jax.random.split(key, 5)
    dense = jax.random.randint(key_dense, (TILES, 1), 0, 8) == 0
    low_counts = jax.random.randint(key_low, (TILES, 8), 1, CAP // 4 + 1)
    high_counts = jax.random.randint(key_high, (TILES, 8), CAP // 2, CAP + 1)
    counts = jnp.where(dense, high_counts, low_counts)
    peak_tile = jax.random.randint(key_peak, (), 0, TILES)
    peak_dir = jax.random.randint(key_dir, (), 0, 8)
    counts = counts.at[peak_tile, peak_dir].set(CAP)
    return counts.astype(jnp.int32)


def set_ends(result, key, least, high):
    place = [jax.random.randint(jax.random.fold_in(key, axis), (), 0, length) for axis, length in enumerate(result.shape)]
    widest = result.shape.index(max(result.shape))
    beside = place[:widest] + [(place[widest] + 1) % result.shape[widest]] + place[widest + 1:]
    return result.at[tuple(place)].set(least).at[tuple(beside)].set(high)


def level_of(rng, extent, cuts, low, top_value):
    def one(dim, blocks):
        steps = jax.random.uniform(jax.random.fold_in(jax.random.fold_in(rng, 6), dim), (blocks,), jnp.float32, low / len(cuts), top_value / len(cuts))
        return jnp.repeat(jnp.exp(steps), extent[dim] // blocks).reshape((-1,) + (1,) * (len(extent) - dim - 1))

    gain = one(*cuts[0])
    for cut in cuts[1:]:
        gain = gain * one(*cut)
    return gain


def scatter_about(rng, shape, scale, most, pieces=(), kind=jnp.bfloat16):
    entries = scale * jax.random.normal(rng, shape, jnp.float32)
    if pieces:
        entries = entries * level_of(rng, shape, pieces, -0.22, 0.18)
    return jnp.clip(entries, -most, most).astype(kind)


def setup_inputs(seed: int = 0) -> dict:
    seeds = jax.random.split(jax.random.key(seed), 10)
    offsets = scatter_about(seeds[0], (V, 3, CELLS), 1.0, 6.0, ((2, 512),))
    metric = jnp.clip(jnp.exp(math.log(3.0) - 2.306499 * jax.random.uniform(seeds[1], (V, CELLS), jnp.float32) ** level_of(seeds[1], (V, CELLS), ((1, 512),), -0.2, 0.2)), 0.29882812, 3.0).astype(jnp.bfloat16)
    centers = scatter_about(seeds[2], (3, CELLS), 1.0, 6.0, ((1, 512),), jnp.float32)
    lap_matrix = scatter_about(seeds[3], (V, V), V ** -0.5, 0.25)
    bend_matrix = scatter_about(seeds[4], (V, V), V ** -0.5, 0.25)
    mig_slots = draw_mig_slots(jax.random.fold_in(seeds[9], 71), 0)
    contact_ids = set_ends(jax.random.randint(seeds[6], (TILES, 8, CAP), 0, CELLS_DEV * NBLK), jax.random.fold_in(seeds[6], 1), 0, (CELLS_DEV * NBLK) - 1).astype(jnp.int32)
    contact_local = set_ends(jax.random.randint(seeds[7], (TILES, 8, CAP), 0, CELLS_DEV), jax.random.fold_in(seeds[7], 1), 0, CELLS_DEV - 1).astype(jnp.int32)
    contact_count = draw_contact_count(jax.random.fold_in(seeds[9], 71), 0)
    return {"offsets": offsets, "metric": metric, "centers": centers, "lap_matrix": lap_matrix, "bend_matrix": bend_matrix, "mig_slots": mig_slots, "contact_ids": contact_ids, "contact_local": contact_local, "contact_count": contact_count}


DIRECTIONS = ((-1, -1), (-1, 0), (-1, 1), (0, -1), (0, 1), (1, -1), (1, 0), (1, 1))
TENSION = 0.5
GAUSS_WIDTH = 4.0
STRENGTH = 8.0
TIME_STEP = 0.25


def membrane(offset_part, metric_part, lap_matrix, bend_matrix):
    cell_count = offset_part.shape[2]
    flattened = offset_part.reshape(V, 3 * cell_count)
    curvature = jnp.dot(lap_matrix, flattened, preferred_element_type=jnp.float32).reshape(V, 3, cell_count)
    metric_col = metric_part.astype(jnp.float32)[:, None, :]
    weighted = (metric_col * curvature).astype(jnp.bfloat16)
    bending = jnp.dot(lap_matrix, weighted.reshape(V, 3 * cell_count), preferred_element_type=jnp.float32).reshape(V, 3, cell_count)
    shear_term = jnp.dot(bend_matrix, flattened, preferred_element_type=jnp.float32).reshape(V, 3, cell_count)
    return metric_col * (TENSION * curvature - bending) - shear_term


def pair_forces(near_rows, far_rows):
    highest = lax.Precision.HIGHEST
    near_sq = jnp.sum(near_rows * near_rows, axis=1)
    far_sq = jnp.sum(far_rows * far_rows, axis=1)
    cross = jnp.einsum("gca,gcv->gav", near_rows, far_rows, precision=highest)
    kernel = jnp.exp(-(near_sq[:, :, None] + far_sq[:, None, :] - 2.0 * cross) / GAUSS_WIDTH)
    row_total = jnp.sum(kernel, axis=2)
    col_total = jnp.sum(kernel, axis=1)
    factor = STRENGTH / VB
    on_near = factor * (near_rows * row_total[:, None, :] - jnp.einsum("gav,gcv->gca", kernel, far_rows, precision=highest))
    on_far = -factor * (jnp.einsum("gav,gca->gcv", kernel, near_rows, precision=highest) - far_rows * col_total[:, None, :])
    return on_near, on_far


def tile_roll(values, along_x, along_y):
    shaped = values.reshape((N_GX, N_GY) + values.shape[1:])
    rolled = jnp.roll(shaped, (along_x, along_y), axis=(0, 1))
    return rolled.reshape(values.shape)


def reference(offsets, metric, centers, lap_matrix, bend_matrix, mig_slots, contact_ids, contact_local, contact_count):
    tile_count = N_GX * N_GY
    position = (centers[None, :, :] + offsets.astype(jnp.float32)).reshape(V, 3, tile_count, CELLS_DEV)

    def tile_force(tile_index):
        offset_part = lax.dynamic_slice_in_dim(offsets, tile_index * CELLS_DEV, CELLS_DEV, 2)
        metric_part = lax.dynamic_slice_in_dim(metric, tile_index * CELLS_DEV, CELLS_DEV, 1)
        return membrane(offset_part, metric_part, lap_matrix, bend_matrix)

    membrane_force = lax.map(tile_force, jnp.arange(tile_count, dtype=jnp.int32))
    membrane_force = jnp.transpose(membrane_force, (1, 2, 0, 3))
    contact = jnp.zeros((V, 3, tile_count, CELLS_DEV), jnp.float32)
    tile_rows = jnp.arange(tile_count, dtype=jnp.int32)[:, None]
    lane_index = jnp.arange(CAP, dtype=jnp.int32)[None, :]
    for heading in range(8):
        step_x, step_y = DIRECTIONS[heading]
        entry_ids = contact_ids[:, heading, :]
        owner_cell = entry_ids // NBLK
        owner_block = entry_ids % NBLK
        blocked = position.reshape(NBLK, VB, 3, tile_count, CELLS_DEV)
        block_rows = jnp.transpose(blocked[owner_block, :, :, tile_rows, owner_cell], (0, 1, 3, 2))
        active = (lane_index < contact_count[:, heading][:, None]).astype(jnp.float32)
        rows_in = tile_roll(block_rows, step_x, step_y)
        active_in = tile_roll(active, step_x, step_y)
        target_slots = contact_local[:, heading, :]
        partner = jnp.transpose(position[:, :, tile_rows, target_slots], (2, 3, 1, 0))

        def per_entry(entry_pair):
            return pair_forces(entry_pair[0], entry_pair[1])

        on_near, on_far = lax.map(per_entry, (jnp.swapaxes(rows_in, 0, 1), jnp.swapaxes(partner, 0, 1)))
        weights_live = jnp.swapaxes(active_in, 0, 1)[:, :, None, None]
        on_near = jnp.swapaxes(on_near * weights_live, 0, 1)
        on_far = jnp.swapaxes(on_far * weights_live, 0, 1)
        contact = contact.at[:, :, tile_rows, target_slots].add(jnp.transpose(on_far, (3, 2, 0, 1)))
        returned = tile_roll(on_near, -step_x, -step_y) * active[:, :, None, None]
        gridded = contact.reshape(NBLK, VB, 3, tile_count, CELLS_DEV)
        gridded = gridded.at[owner_block, :, :, tile_rows, owner_cell].add(jnp.transpose(returned, (0, 1, 3, 2)))
        contact = gridded.reshape(V, 3, tile_count, CELLS_DEV)
    displaced = position + TIME_STEP * (membrane_force + contact)
    metric_wide = metric.astype(jnp.float32).reshape(V, tile_count, CELLS_DEV)
    settled = displaced
    metric_settled = metric_wide
    for heading in range(8):
        step_x, step_y = DIRECTIONS[heading]
        target_slots = mig_slots[:, heading, :]
        leaving = jnp.transpose(displaced[:, :, tile_rows, target_slots], (2, 0, 1, 3))
        leaving_metric = jnp.transpose(metric_wide[:, tile_rows, target_slots], (1, 0, 2))
        arriving = tile_roll(leaving, step_x, step_y)
        arriving_metric = tile_roll(leaving_metric, step_x, step_y)
        settled = settled.at[:, :, tile_rows, target_slots].set(jnp.transpose(arriving, (1, 2, 0, 3)))
        metric_settled = metric_settled.at[:, tile_rows, target_slots].set(jnp.transpose(arriving_metric, (1, 0, 2)))
    new_centers = jnp.mean(settled, axis=0)
    new_offsets = (settled - new_centers[None]).astype(jnp.bfloat16)
    total = tile_count * CELLS_DEV
    return (new_offsets.reshape(V, 3, total), metric_settled.astype(jnp.bfloat16).reshape(V, total), new_centers.reshape(3, total))
```

```python
import functools

import jax
import jax.numpy as jnp
from jax import lax
from jax.experimental import pallas as pl
from jax.experimental.pallas import tpu as pltpu
from jax.sharding import PartitionSpec as P

V = 642
NBLK = 6
VB = 107
LANES = 128
CAP = 4
VPAD = 768
HEADINGS = 8

DIRECTIONS = ((-1, -1), (-1, 0), (-1, 1), (0, -1), (0, 1), (1, -1), (1, 0), (1, 1))
TENSION = 0.5
TIME_STEP = 0.25
FACTOR = 8.0 / VB
LOG2E = 1.4426950408889634
OFF = 1.0e6
MESH = pl.DeviceIdType.MESH
F32 = jnp.float32
BF16 = jnp.bfloat16


def mm(a, b):
    return lax.dot_general(a, b, (((1,), (0,)), ((), ())), preferred_element_type=F32)


def mm_nt(a, b):
    return lax.dot_general(a, b, (((1,), (1,)), ((), ())), preferred_element_type=F32)


def two_pieces(x):
    hi = x.astype(BF16)
    lo = (x - hi.astype(F32)).astype(BF16)
    return hi, lo


def three_pieces(x):
    hi = x.astype(BF16)
    rest = x - hi.astype(F32)
    mid = rest.astype(BF16)
    lo = (rest - mid.astype(F32)).astype(BF16)
    return hi, mid, lo


def id_table(ref):
    sub = lax.broadcasted_iota(jnp.int32, (8, LANES), 0) & 3
    tiles = []
    for h in range(HEADINGS):
        tile = jnp.where(
            sub == 0, ref[0, h], jnp.where(sub == 1, ref[1, h], jnp.where(sub == 2, ref[2, h], ref[3, h]))
        )
        tiles += [tile, tile]
    return jnp.concatenate(tiles, axis=0)


def kernel(
    n_gx, n_gy,
    x_hbm, met_hbm, cen_hbm, lap_hbm, bend_hbm, mig_s, ids_s, loc_s, cnt_s,
    off_o, met_o, cen_o,
    x, met, cen, lap, bend, wide, row_s, row_r, near_s, near_r, cell_s, cell_r,
    bt, qt, w, pp, disp, in_sem, send_sem, recv_sem,
):
    gx, gy = lax.axis_index("gx"), lax.axis_index("gy")

    def neighbour(h, sign):
        dx, dy = DIRECTIONS[h]
        return (
            lax.rem(gx + (sign * dx + n_gx), n_gx),
            lax.rem(gy + (sign * dy + n_gy), n_gy),
        )

    barrier = pltpu.get_barrier_semaphore()
    for h in range(HEADINGS):
        pl.semaphore_signal(barrier, inc=1, device_id=neighbour(h, 1), device_id_type=MESH)

    loads = [
        pltpu.make_async_copy(src, dst, in_sem.at[i])
        for i, (src, dst) in enumerate(
            ((x_hbm, x), (cen_hbm, cen), (met_hbm, met), (lap_hbm, lap), (bend_hbm, bend))
        )
    ]
    for load in loads:
        load.start()

    def send(kind, src, dst, h, sign):
        rows = pl.ds(16 * h, 16)
        return pltpu.make_async_remote_copy(
            src_ref=src.at[rows],
            dst_ref=dst.at[rows],
            send_sem=send_sem.at[kind, h],
            recv_sem=recv_sem.at[kind, h],
            device_id=neighbour(h, sign),
            device_id_type=MESH,
        )

    row = lax.broadcasted_iota(jnp.int32, (LANES, LANES), 0)
    lane = lax.broadcasted_iota(jnp.int32, (LANES, LANES), 1)
    rk = (row >> 2) & 3
    rj = row & 3

    def spread(one_hot, ks):
        return jnp.concatenate([jnp.where(rk == k, one_hot, 0.0) for k in ks], axis=1)

    ids = id_table(ids_s)
    owner = (ids * 10923) >> 16
    block = ids - NBLK * owner
    own_hot = (lane == owner).astype(F32)
    loc_hot = (lane == id_table(loc_s)).astype(F32)
    mig_hot = (lane == id_table(mig_s)).astype(F32)
    counts = jnp.concatenate(
        [jnp.full((16, LANES), cnt_s[0, h], jnp.int32) for h in range(HEADINGS)], axis=0
    )
    live = (rj < counts) & (lane < VB)

    loads[0].wait()
    loads[1].wait()
    x0, x1, x2 = x[0], x[1], x[2]
    xcat = jnp.concatenate([x0, x1, x2], axis=1)
    cen_rows = jnp.where(rk == 0, cen[0:1, :], jnp.where(rk == 1, cen[1:2, :], cen[2:3, :]))
    cen_rows = jnp.where(rk == 3, 0.0, cen_rows)
    wide[:, VPAD - LANES:] = jnp.zeros((LANES, LANES), F32)
    wide[:, :V] = mm_nt(spread(own_hot, (0, 1, 2)).astype(BF16), xcat)
    picked = jnp.zeros((LANES, LANES), F32)
    for b in range(NBLK):
        tile, shift = divmod(VB * b, LANES)
        two = wide[:, tile * LANES:(tile + 2) * LANES]
        if shift:
            two = pltpu.roll(two, 2 * LANES - shift, 1)
        picked = jnp.where(block == b, two[:, :LANES], picked)
    own_cen = jnp.sum(own_hot * cen_rows, axis=1, keepdims=True)
    row_s[...] = jnp.where(live, jnp.where(rk == 3, 1.0, picked + own_cen), 0.0)

    pl.semaphore_wait(barrier, HEADINGS)
    row_sends = [send(0, row_s, row_r, h, 1) for h in range(HEADINGS)]
    for copy in row_sends:
        copy.start()

    loc_spread = spread(loc_hot, (0, 1, 2)).astype(BF16)
    f0, f1, f2 = x0.astype(F32), x1.astype(F32), x2.astype(F32)
    sq = (f0 * f0 + f1 * f1 + f2 * f2) * (-0.25 * LOG2E)
    source = jnp.concatenate([x0, x1, x2, *three_pieces(sq)], axis=1)
    none = jnp.zeros((LANES, 3 * LANES), BF16)
    take_q = jnp.concatenate([loc_spread, none], axis=1)
    take_sq = jnp.concatenate([none, loc_spread], axis=1)
    parts = []
    for h in range(HEADINGS):
        rows = slice(16 * h, 16 * h + 16)
        parts += [take_q[rows], take_q[rows], take_q[rows], take_sq[rows]]
    take = jnp.concatenate(parts, axis=0)
    col = lax.broadcasted_iota(jnp.int32, (1, 512), 1)
    ones_col = jnp.where((((col >> 4) & 3) < 3) & (((col >> 2) & 3) == 3), 1.0, 0.0)
    bt[...] = (mm_nt(source, take) + ones_col).astype(BF16)
    ones_row = jnp.where(rk == 3, 1.0, 0.0)[:, :1]
    qt[...] = (mm_nt(loc_spread, xcat) + ones_row).astype(BF16)
    loc_cen = jnp.sum(loc_hot * cen_rows, axis=1, keepdims=True)

    loads[2].wait()
    loads[3].wait()
    loads[4].wait()
    metric = met[...]
    m1 = metric.astype(F32)
    m3 = jnp.concatenate([m1, m1, m1], axis=1)
    curvature = mm(lap[...], xcat)
    weighted = (m3 * curvature).astype(BF16)
    force = m3 * (TENSION * curvature - mm(lap[...], weighted)) - mm(bend[...], xcat)
    cen3 = jnp.concatenate([cen[0:1, :], cen[1:2, :], cen[2:3, :]], axis=1)
    xf = jnp.concatenate([f0, f1, f2], axis=1)
    disp[...] = xf + cen3 + TIME_STEP * force

    for copy in row_sends:
        copy.wait()

    got = row_r[...]
    rel = got - loc_cen
    rel_sq = jnp.where(rk == 3, 0.0, rel * rel)
    tot = pltpu.roll(rel_sq, 4, 0) + pltpu.roll(rel_sq, 8, 0) + pltpu.roll(rel_sq, 12, 0)
    vals = jnp.where(
        rk == 3, (-0.25 * LOG2E) * tot - OFF * (1.0 - got), (0.5 * LOG2E) * rel
    )
    v0, v1, v2 = three_pieces(vals)
    one16 = jnp.ones((16, LANES), BF16)
    near_sends = []
    for t in range(4):
        blocks = []
        for h in (2 * t, 2 * t + 1):
            rows = slice(16 * h, 16 * h + 16)
            blocks += [v0[rows], v1[rows], v2[rows], one16]
        base = jnp.concatenate(blocks, axis=0)
        left = bt[:, t * LANES:(t + 1) * LANES]
        for q in range(4):
            right = jnp.concatenate(
                [
                    jnp.where(((row >> 6) == (q // 2)) & (rj == 2 * (q % 2) + i), base, jnp.zeros_like(base))
                    for i in range(2)
                ],
                axis=1,
            )
            at = (t * 4 + q) * 256
            w[:, at:at + 256] = jnp.exp2(mm(left, right)).astype(BF16)
        rj16 = lax.broadcasted_iota(jnp.int32, (16, LANES), 0) & 3
        sums = []
        for h in (2 * t, 2 * t + 1):
            all4 = mm(qt[16 * h:16 * h + 16, :], w[:, 512 * h:512 * h + 512])
            mine = all4[:, :LANES]
            for j in range(1, 4):
                mine = jnp.where(rj16 == j, all4[:, j * LANES:(j + 1) * LANES], mine)
            sums.append(mine)
        total = jnp.concatenate(sums, axis=0)
        rk32 = rk[:32]
        weight = jnp.where(
            rk32 == 0,
            pltpu.roll(total, 20, 0),
            jnp.where(rk32 == 1, pltpu.roll(total, 24, 0), pltpu.roll(total, 28, 0)),
        )
        rows = slice(32 * t, 32 * t + 32)
        near_s[rows, :] = FACTOR * (rel[rows] * weight - total)
        for h in (2 * t, 2 * t + 1):
            copy = send(1, near_s, near_r, h, -1)
            copy.start()
            near_sends.append(copy)

    rel_t = jnp.transpose(jnp.where(rk == 3, 1.0, rel))
    rel_hi, rel_lo = two_pieces(rel_t)
    rel2 = jnp.concatenate([rel_hi, rel_lo], axis=1)
    lane2 = lax.broadcasted_iota(jnp.int32, (LANES, 2 * LANES), 1) & 127
    for h in range(HEADINGS):
        for j in range(CAP):
            at = (4 * h + j) * LANES
            pp[at:at + LANES, :] = jnp.where(
                ((lane2 >> 4) == h) & ((lane2 & 3) == j), rel2, jnp.zeros_like(rel2)
            )
    far2 = mm(w[...], pp[...])
    far = jnp.concatenate(two_pieces(far2[:, :LANES] + far2[:, LANES:]), axis=1)
    loc_put = spread(loc_hot, (0, 1, 2, 3)).astype(BF16)
    put = mm(far, jnp.concatenate([loc_put, loc_put], axis=0))
    put3 = put[:, 3 * LANES:]
    weight3 = jnp.concatenate([put3, put3, put3], axis=1)
    disp[...] = disp[...] - (TIME_STEP * FACTOR) * (put[:, :3 * LANES] - xf * weight3)

    own_spread = spread(own_hot, (0, 1, 2))
    block3 = jnp.concatenate([block, block, block], axis=1)
    near_put = jnp.concatenate(
        [jnp.where(block3 == b, own_spread, 0.0).astype(BF16) for b in range(NBLK)], axis=1
    )
    near_put = jnp.concatenate([near_put, near_put], axis=0)

    for copy in near_sends:
        copy.wait()
    near = jnp.concatenate(two_pieces(jnp.transpose(near_r[...])), axis=1)
    back = mm(near, near_put)
    for b in range(NBLK):
        rows = slice(VB * b, VB * b + VB)
        disp[rows, :] = disp[rows, :] + TIME_STEP * back[:VB, 384 * b:384 * b + 384]

    d_hi, d_lo = two_pieces(disp[...])
    moving = jnp.concatenate([d_hi, d_lo, metric], axis=1)
    pick3 = spread(mig_hot, (0, 1, 2))
    pick = jnp.concatenate([pick3, pick3, jnp.where(rk == 3, mig_hot, 0.0)], axis=1).astype(BF16)
    cell_s[:, VPAD - LANES:] = jnp.zeros((LANES, LANES), F32)
    cell_s[:, :V] = mm_nt(pick, moving)
    cell_sends = [send(2, cell_s, cell_r, h, 1) for h in range(HEADINGS)]
    for copy in cell_sends:
        copy.start()

    keep = 1.0 - jnp.sum(jnp.where(rk == 0, mig_hot, 0.0), axis=0, keepdims=True)
    keep3 = jnp.concatenate([keep, keep, keep], axis=1)
    mig_put = spread(mig_hot, (0, 1, 2, 3)).astype(BF16)
    mig_put = jnp.concatenate([mig_put, mig_put], axis=0)
    for copy in cell_sends:
        copy.wait()
    come = jnp.transpose(cell_r[...])[:V]
    arrived = mm(jnp.concatenate(two_pieces(come), axis=1), mig_put)
    met_o[...] = (m1 * keep + arrived[:, 3 * LANES:]).astype(BF16)
    settled = disp[...] * keep3 + arrived[:, :3 * LANES]
    centre = jnp.sum(settled, axis=0, keepdims=True) * (1.0 / V)
    offs = (settled - centre).astype(BF16)
    for k in range(3):
        off_o[k] = offs[:, k * LANES:(k + 1) * LANES]
        cen_o[k:k + 1, :] = centre[:, k * LANES:(k + 1) * LANES]


def solution(mesh):
    n_gx, n_gy = mesh.shape["gx"], mesh.shape["gy"]

    def per_device(offsets, metric, centers, lap, bend, mig_slots, contact_ids, contact_local, contact_count):
        hbm = pl.BlockSpec(memory_space=pl.ANY)
        smem = pl.BlockSpec(memory_space=pltpu.SMEM)
        vmem = pl.BlockSpec(memory_space=pltpu.VMEM)
        offs, met, cen = pl.pallas_call(
            functools.partial(kernel, n_gx, n_gy),
            out_shape=(
                jax.ShapeDtypeStruct((3, V, LANES), BF16),
                jax.ShapeDtypeStruct((V, LANES), BF16),
                jax.ShapeDtypeStruct((3, LANES), F32),
            ),
            in_specs=[hbm] * 5 + [smem] * 4,
            out_specs=(vmem, vmem, vmem),
            scratch_shapes=[
                pltpu.VMEM((3, V, LANES), BF16),
                pltpu.VMEM((V, LANES), BF16),
                pltpu.VMEM((3, LANES), F32),
                pltpu.VMEM((V, V), BF16),
                pltpu.VMEM((V, V), BF16),
                pltpu.VMEM((LANES, VPAD), F32),
                pltpu.VMEM((LANES, LANES), F32),
                pltpu.VMEM((LANES, LANES), F32),
                pltpu.VMEM((LANES, LANES), F32),
                pltpu.VMEM((LANES, LANES), F32),
                pltpu.VMEM((LANES, VPAD), F32),
                pltpu.VMEM((LANES, VPAD), F32),
                pltpu.VMEM((V, 512), BF16),
                pltpu.VMEM((LANES, V), BF16),
                pltpu.VMEM((V, 32 * LANES), BF16),
                pltpu.VMEM((32 * LANES, 2 * LANES), BF16),
                pltpu.VMEM((V, 3 * LANES), F32),
                pltpu.SemaphoreType.DMA((5,)),
                pltpu.SemaphoreType.DMA((3, HEADINGS)),
                pltpu.SemaphoreType.DMA((3, HEADINGS)),
            ],
            compiler_params=pltpu.CompilerParams(
                collective_id=0, has_side_effects=True, vmem_limit_bytes=56 * 1024 * 1024
            ),
        )(
            jnp.transpose(offsets, (1, 0, 2)),
            metric,
            centers,
            lap,
            bend,
            jnp.transpose(mig_slots[0]),
            jnp.transpose(contact_ids[0]),
            jnp.transpose(contact_local[0]),
            contact_count,
        )
        return jnp.transpose(offs, (1, 0, 2)), met, cen

    return jax.shard_map(
        per_device,
        mesh=mesh,
        in_specs=(
            P(None, None, ("gx", "gy")),
            P(None, ("gx", "gy")),
            P(None, ("gx", "gy")),
            P(),
            P(),
            P(("gx", "gy"), None, None),
            P(("gx", "gy"), None, None),
            P(("gx", "gy"), None, None),
            P(("gx", "gy"), None),
        ),
        out_specs=(P(None, None, ("gx", "gy")), P(None, ("gx", "gy")), P(None, ("gx", "gy"))),
        check_vma=False,
    )
```

```python
import functools

import jax
import jax.numpy as jnp
from jax import lax
from jax.experimental import pallas as pl
from jax.experimental.pallas import tpu as pltpu
from jax.sharding import PartitionSpec as P

V = 642
NBLK = 6
VB = 107
LANES = 128
CAP = 4
VPAD = 768
HALF = 384
HEADINGS = 8

DIRECTIONS = ((-1, -1), (-1, 0), (-1, 1), (0, -1), (0, 1), (1, -1), (1, 0), (1, 1))
TENSION = 0.5
TIME_STEP = 0.25
FACTOR = 8.0 / VB
LOG2E = 1.4426950408889634
OFF = 1.0e6
MESH = pl.DeviceIdType.MESH
F32 = jnp.float32
BF16 = jnp.bfloat16


def mm(a, b):
    return lax.dot_general(a, b, (((1,), (0,)), ((), ())), preferred_element_type=F32)


def mm_nt(a, b):
    return lax.dot_general(a, b, (((1,), (1,)), ((), ())), preferred_element_type=F32)


def two_pieces(x):
    hi = x.astype(BF16)
    lo = (x - hi.astype(F32)).astype(BF16)
    return hi, lo


def three_pieces(x):
    hi = x.astype(BF16)
    rest = x - hi.astype(F32)
    mid = rest.astype(BF16)
    lo = (rest - mid.astype(F32)).astype(BF16)
    return hi, mid, lo


def id_table(ref, times):
    sub = lax.broadcasted_iota(jnp.int32, (8, LANES), 0) & 3
    tiles = []
    for h in range(HEADINGS):
        tile = jnp.where(
            sub == 0, ref[0, h], jnp.where(sub == 1, ref[1, h], jnp.where(sub == 2, ref[2, h], ref[3, h]))
        )
        tiles += [tile] * times
    return jnp.concatenate(tiles, axis=0)


def kernel(
    n_gx, n_gy,
    x_hbm, met_hbm, cen_hbm, lap_hbm, bend_hbm, mig_s, ids_s, loc_s, cnt_s,
    stay_o, come_o, met_come_o, put_o, put_met_o,
    x, met, cen, lap, bend, wide, row_s, row_r, near_s, near_r, cell_s, cell_r, wide2, met_out, met_in,
    bt, qt, w, pp, disp, frame, rel_s, in_sem, send_sem, recv_sem,
):
    gx, gy = lax.axis_index("gx"), lax.axis_index("gy")

    def neighbour(h, sign):
        nth = h + lax.div(h + 4, 8)
        dx, dy = lax.div(nth, 3) - 1, lax.rem(nth, 3) - 1
        return (
            lax.rem(gx + (sign * dx + n_gx), n_gx),
            lax.rem(gy + (sign * dy + n_gy), n_gy),
        )

    barrier = pltpu.get_barrier_semaphore()
    for h in range(HEADINGS):
        pl.semaphore_signal(barrier, inc=1, device_id=neighbour(h, 1), device_id_type=MESH)

    loads = [
        pltpu.make_async_copy(src, dst, in_sem.at[i])
        for i, (src, dst) in enumerate(
            ((x_hbm, x), (cen_hbm, cen), (met_hbm, met), (lap_hbm, lap), (bend_hbm, bend))
        )
    ]
    for load in loads:
        load.start()

    def send(kind, src, dst, h, sign, count=16):
        rows = pl.ds(count * h, count)
        return pltpu.make_async_remote_copy(
            src_ref=src.at[rows],
            dst_ref=dst.at[rows],
            send_sem=send_sem.at[kind, h],
            recv_sem=recv_sem.at[kind, h],
            device_id=neighbour(h, sign),
            device_id_type=MESH,
        )

    row = lax.broadcasted_iota(jnp.int32, (LANES, LANES), 0)
    lane = lax.broadcasted_iota(jnp.int32, (LANES, LANES), 1)
    rk = (row >> 2) & 3
    rj = row & 3

    def spread(one_hot, ks):
        return jnp.concatenate([jnp.where(rk == k, one_hot, 0.0) for k in ks], axis=1)

    ids = id_table(ids_s, 2)
    owner = (ids * 10923) >> 16
    block = ids - NBLK * owner
    own_hot = (lane == owner).astype(F32)
    loc_hot = (lane == id_table(loc_s, 2)).astype(F32)

    def rows_lanes(rows):
        shape = (rows, LANES)
        return lax.broadcasted_iota(jnp.int32, shape, 0), lax.broadcasted_iota(jnp.int32, shape, 1)

    row64, lane64 = rows_lanes(64)
    row192, lane192 = rows_lanes(192)
    late64 = (row64 & 4) == 4
    late192 = (row192 & 4) == 4
    tile192 = row192 >> 3
    k192 = tile192 - 3 * ((tile192 * 171) >> 9)
    met_hot = (lane64 == id_table(mig_s, 1)).astype(F32)
    mig_hot = (lane192 == id_table(mig_s, 3)).astype(F32)

    def halves(full, late):
        late3 = jnp.concatenate([late, late, late], axis=1)
        return jnp.where(late3, full[:, HALF:], full[:, :HALF])

    counts = jnp.concatenate(
        [jnp.full((16, LANES), cnt_s[0, h], jnp.int32) for h in range(HEADINGS)], axis=0
    )
    live = (rj < counts) & (lane < VB)

    loads[0].wait()
    loads[1].wait()
    x0, x1, x2 = x[0], x[1], x[2]
    xcat = jnp.concatenate([x0, x1, x2], axis=1)
    cen_rows = jnp.where(rk == 0, cen[0:1, :], jnp.where(rk == 1, cen[1:2, :], cen[2:3, :]))
    cen_rows = jnp.where(rk == 3, 0.0, cen_rows)
    wide[:, VPAD - LANES:] = jnp.zeros((LANES, LANES), F32)
    wide[:, :V] = mm_nt(spread(own_hot, (0, 1, 2)).astype(BF16), xcat)
    picked = jnp.zeros((LANES, LANES), F32)
    for b in range(NBLK):
        tile, shift = divmod(VB * b, LANES)
        two = wide[:, tile * LANES:(tile + 2) * LANES]
        if shift:
            two = pltpu.roll(two, 2 * LANES - shift, 1)
        picked = jnp.where(block == b, two[:, :LANES], picked)
    own_cen = jnp.sum(own_hot * cen_rows, axis=1, keepdims=True)
    row_s[...] = jnp.where(live, jnp.where(rk == 3, 1.0, picked + own_cen), 0.0)

    pl.semaphore_wait(barrier, HEADINGS)
    row_sends = [send(0, row_s, row_r, h, 1) for h in range(HEADINGS)]
    for copy in row_sends:
        copy.start()

    loads[2].wait()
    metric = met[...]
    wide2[:, VPAD - LANES:] = jnp.zeros((192, LANES), F32)
    wide2[:64, :V] = mm_nt(met_hot.astype(BF16), metric)
    met_out[...] = halves(wide2[:64, :], late64)
    metric_sends = [send(3, met_out, met_in, h, 1, 8) for h in range(HEADINGS)]
    for copy in metric_sends:
        copy.start()

    loc_spread = spread(loc_hot, (0, 1, 2)).astype(BF16)
    f0, f1, f2 = x0.astype(F32), x1.astype(F32), x2.astype(F32)
    sq = (f0 * f0 + f1 * f1 + f2 * f2) * (-0.25 * LOG2E)
    source = jnp.concatenate([x0, x1, x2, *three_pieces(sq)], axis=1)
    none = jnp.zeros((LANES, 3 * LANES), BF16)
    take_q = jnp.concatenate([loc_spread, none], axis=1)
    take_sq = jnp.concatenate([none, loc_spread], axis=1)
    parts = []
    for h in range(HEADINGS):
        rows = slice(16 * h, 16 * h + 16)
        parts += [take_q[rows], take_q[rows], take_q[rows], take_sq[rows]]
    take = jnp.concatenate(parts, axis=0)
    col = lax.broadcasted_iota(jnp.int32, (1, 512), 1)
    ones_col = jnp.where((((col >> 4) & 3) < 3) & (((col >> 2) & 3) == 3), 1.0, 0.0)
    bt[...] = (mm_nt(source, take) + ones_col).astype(BF16)
    ones_row = jnp.where(rk == 3, 1.0, 0.0)[:, :1]
    qt[...] = (mm_nt(loc_spread, xcat) + ones_row).astype(BF16)
    frame[...] = jnp.broadcast_to(jnp.sum(loc_hot * cen_rows, axis=1, keepdims=True), (LANES, LANES))

    loads[3].wait()
    loads[4].wait()
    m1 = metric.astype(F32)
    m3 = jnp.concatenate([m1, m1, m1], axis=1)
    curvature = mm(lap[...], xcat)
    weighted = (m3 * curvature).astype(BF16)
    force = m3 * (TENSION * curvature - mm(lap[...], weighted)) - mm(bend[...], xcat)
    cen3 = jnp.concatenate([cen[0:1, :], cen[1:2, :], cen[2:3, :]], axis=1)
    xf = jnp.concatenate([f0, f1, f2], axis=1)
    disp[...] = xf + cen3 + TIME_STEP * force

    one16 = jnp.ones((16, LANES), BF16)
    row32, rk32 = row[:32], rk[:32]
    rj16 = rj[:16]
    backwards = lax.rem(gx + 1, n_gx // 2) == 0
    near_sends = []
    for step in range(4):
        t = jnp.where(backwards, 3 - step, step)
        for i in range(2):
            send(0, row_s, row_r, 2 * t + i, 1).wait_recv()
        rows = pl.ds(pl.multiple_of(32 * t, 32), 32)
        got = row_r[rows, :]
        rel = got - frame[rows, :]
        rel_s[rows, :] = rel
        rel_sq = jnp.where(rk32 == 3, 0.0, rel * rel)
        tot = pltpu.roll(rel_sq, 4, 0) + pltpu.roll(rel_sq, 8, 0) + pltpu.roll(rel_sq, 12, 0)
        vals = jnp.where(
            rk32 == 3, (-0.25 * LOG2E) * tot - OFF * (1.0 - got), (0.5 * LOG2E) * rel
        )
        v0, v1, v2 = three_pieces(vals)
        base = jnp.concatenate(
            [v0[:16], v1[:16], v2[:16], one16, v0[16:], v1[16:], v2[16:], one16], axis=0
        )
        left = bt[:, pl.ds(pl.multiple_of(t * LANES, LANES), LANES)]
        weights = []
        for q in range(4):
            right = jnp.concatenate(
                [
                    jnp.where(((row >> 6) == (q // 2)) & (rj == 2 * (q % 2) + i), base, jnp.zeros_like(base))
                    for i in range(2)
                ],
                axis=1,
            )
            pair = jnp.exp2(mm(left, right)).astype(BF16)
            w[:, pl.ds(pl.multiple_of(1024 * t + 256 * q, 256), 256)] = pair
            weights.append(pair)
        sums = []
        for i in range(2):
            mine = None
            partner = qt[pl.ds(pl.multiple_of(32 * t + 16 * i, 16), 16), :]
            for j2 in range(2):
                two = mm(partner, weights[2 * i + j2])
                for j in range(2):
                    part = two[:, j * LANES:(j + 1) * LANES]
                    mine = part if mine is None else jnp.where(rj16 == 2 * j2 + j, part, mine)
            sums.append(mine)
        total = jnp.concatenate(sums, axis=0)
        weight = jnp.where(
            rk32 == 0,
            pltpu.roll(total, 20, 0),
            jnp.where(rk32 == 1, pltpu.roll(total, 24, 0), pltpu.roll(total, 28, 0)),
        )
        near_s[rows, :] = FACTOR * (rel * weight - total)
        for i in range(2):
            copy = send(1, near_s, near_r, 2 * t + i, -1)
            copy.start()
            near_sends.append(copy)
    for copy in row_sends:
        copy.wait_send()

    rel_t = jnp.transpose(jnp.where(rk == 3, 1.0, rel_s[...]))
    rel_hi, rel_lo = two_pieces(rel_t)
    rel2 = jnp.concatenate([rel_hi, rel_lo], axis=1)
    lane2 = lax.broadcasted_iota(jnp.int32, (LANES, 2 * LANES), 1) & 127
    for h in range(HEADINGS):
        for j in range(CAP):
            at = (4 * h + j) * LANES
            pp[at:at + LANES, :] = jnp.where(
                ((lane2 >> 4) == h) & ((lane2 & 3) == j), rel2, jnp.zeros_like(rel2)
            )
    far2 = mm(w[...], pp[...])
    far = jnp.concatenate(two_pieces(far2[:, :LANES] + far2[:, LANES:]), axis=1)
    loc_put = spread(loc_hot, (0, 1, 2, 3)).astype(BF16)
    put = mm(far, jnp.concatenate([loc_put, loc_put], axis=0))
    put3 = put[:, 3 * LANES:]
    weight3 = jnp.concatenate([put3, put3, put3], axis=1)
    disp[...] = disp[...] - (TIME_STEP * FACTOR) * (put[:, :3 * LANES] - xf * weight3)

    pick3 = jnp.concatenate([jnp.where(k192 == k, mig_hot, 0.0) for k in range(3)], axis=1).astype(BF16)
    pick = jnp.concatenate([pick3, pick3], axis=1)
    wide2[:, :V] = mm_nt(pick, jnp.concatenate(two_pieces(disp[...]), axis=1))
    leave = halves(wide2[...], late192)
    own_spread = spread(own_hot, (0, 1, 2))
    own_b16 = own_spread.astype(BF16)
    same = (TIME_STEP * mm_nt(pick3, own_b16)).astype(BF16)
    same = jnp.concatenate([same, same], axis=1)
    block3 = jnp.concatenate([block, block, block], axis=1)
    near_put = jnp.concatenate(
        [jnp.where(block3 == b, own_spread, 0.0).astype(BF16) for b in range(NBLK)], axis=1
    )
    near_put = jnp.concatenate([near_put, near_put], axis=0)

    for copy in near_sends:
        copy.wait()
    near = jnp.where(rk == 3, 0.0, near_r[...])
    places = [jnp.zeros((LANES, LANES), F32) for _ in range(VPAD // LANES)]
    for b in range(NBLK):
        tile, shift = divmod(VB * b, LANES)
        piece = jnp.where((block == b) & (lane < VB), near, 0.0)
        if shift:
            piece = pltpu.roll(piece, shift, 1)
            places[tile + 1] = places[tile + 1] + jnp.where(lane < shift, piece, 0.0)
            piece = jnp.where(lane >= shift, piece, 0.0)
        places[tile] = places[tile] + piece
    placed = jnp.concatenate(places, axis=1)
    cell_s[...] = leave + halves(mm(same, jnp.concatenate(two_pieces(placed), axis=0)), late192)
    cell_sends = [send(2, cell_s, cell_r, h, 1, 24) for h in range(HEADINGS)]
    for copy in cell_sends:
        copy.start()

    near_t = jnp.concatenate(two_pieces(jnp.transpose(near)), axis=1)
    back = mm(near_t, near_put)
    for b in range(NBLK):
        rows = slice(VB * b, VB * b + VB)
        disp[rows, :] = disp[rows, :] + TIME_STEP * back[:VB, 384 * b:384 * b + 384]
    keep = 1.0 - jnp.sum(jnp.where(late64, 0.0, met_hot), axis=0, keepdims=True)
    keep3 = jnp.concatenate([keep, keep, keep], axis=1)
    stay_o[:, :3 * LANES] = disp[...] * keep3
    stay_o[:, 3 * LANES:] = m1 * keep
    late3 = jnp.concatenate([late192, late192, late192], axis=1)
    for half in range(2):
        put = jnp.where(late3 == (half == 1), pick3, jnp.zeros_like(pick3))
        put_o[half] = jnp.concatenate([put, put], axis=0)
        put_met_o[half] = jnp.where(late64 == (half == 1), met_hot, 0.0).astype(BF16)
    for copy in metric_sends:
        copy.wait()
    met_come_o[...] = met_in[...]
    for copy in cell_sends:
        copy.wait()
    come_o[...] = cell_r[...]


def settle(stay, come, met_come, put, put_met, off_o, met_o, cen_o):
    met_cells = jnp.transpose(met_come[...]).astype(BF16)
    met_in = jnp.concatenate([mm(met_cells, put_met[0]), mm(met_cells, put_met[1])], axis=0)[:V]
    met_o[...] = (stay[:, 3 * LANES:] + met_in).astype(BF16)
    cells = jnp.concatenate(two_pieces(jnp.transpose(come[...])), axis=1)
    arrived = jnp.concatenate([mm(cells, put[0]), mm(cells, put[1])], axis=0)[:V]
    settled = stay[:, :3 * LANES] + arrived
    centre = jnp.sum(settled, axis=0, keepdims=True) * (1.0 / V)
    offs = (settled - centre).astype(BF16)
    for k in range(3):
        off_o[k] = offs[:, k * LANES:(k + 1) * LANES]
        cen_o[k:k + 1, :] = centre[:, k * LANES:(k + 1) * LANES]


def solution(mesh):
    n_gx, n_gy = mesh.shape["gx"], mesh.shape["gy"]

    def per_device(offsets, metric, centers, lap, bend, mig_slots, contact_ids, contact_local, contact_count):
        hbm = pl.BlockSpec(memory_space=pltpu.HBM)
        smem = pl.BlockSpec(memory_space=pltpu.SMEM)
        vmem = pl.BlockSpec(memory_space=pltpu.VMEM)
        parts = pl.pallas_call(
            functools.partial(kernel, n_gx, n_gy),
            out_shape=(
                pltpu.VMEM((V, 4 * LANES), F32),
                pltpu.VMEM((192, HALF), F32),
                pltpu.VMEM((64, HALF), F32),
                pltpu.VMEM((2, HALF, 3 * LANES), BF16),
                pltpu.VMEM((2, 64, LANES), BF16),
            ),
            in_specs=[hbm] * 5 + [smem] * 4,
            out_specs=(vmem,) * 5,
            scratch_shapes=[
                pltpu.VMEM((3, V, LANES), BF16),
                pltpu.VMEM((V, LANES), BF16),
                pltpu.VMEM((3, LANES), F32),
                pltpu.VMEM((V, V), BF16),
                pltpu.VMEM((V, V), BF16),
                pltpu.VMEM((LANES, VPAD), F32),
                pltpu.VMEM((LANES, LANES), F32),
                pltpu.VMEM((LANES, LANES), F32),
                pltpu.VMEM((LANES, LANES), F32),
                pltpu.VMEM((LANES, LANES), F32),
                pltpu.VMEM((192, HALF), F32),
                pltpu.VMEM((192, HALF), F32),
                pltpu.VMEM((192, VPAD), F32),
                pltpu.VMEM((64, HALF), F32),
                pltpu.VMEM((64, HALF), F32),
                pltpu.VMEM((V, 512), BF16),
                pltpu.VMEM((LANES, V), BF16),
                pltpu.VMEM((V, 32 * LANES), BF16),
                pltpu.VMEM((32 * LANES, 2 * LANES), BF16),
                pltpu.VMEM((V, 3 * LANES), F32),
                pltpu.VMEM((LANES, LANES), F32),
                pltpu.VMEM((LANES, LANES), F32),
                pltpu.SemaphoreType.DMA((5,)),
                pltpu.SemaphoreType.DMA((4, HEADINGS)),
                pltpu.SemaphoreType.DMA((4, HEADINGS)),
            ],
            compiler_params=pltpu.CompilerParams(
                collective_id=0, has_side_effects=True, vmem_limit_bytes=58 * 1024 * 1024
            ),
        )(
            jnp.transpose(offsets, (1, 0, 2)),
            metric,
            centers,
            lap,
            bend,
            jnp.transpose(mig_slots[0]),
            jnp.transpose(contact_ids[0]),
            jnp.transpose(contact_local[0]),
            contact_count,
        )
        offs, met, cen = pl.pallas_call(
            settle,
            out_shape=(
                jax.ShapeDtypeStruct((3, V, LANES), BF16),
                jax.ShapeDtypeStruct((V, LANES), BF16),
                jax.ShapeDtypeStruct((3, LANES), F32),
            ),
            in_specs=[vmem] * 5,
            out_specs=(vmem, vmem, vmem),
            compiler_params=pltpu.CompilerParams(vmem_limit_bytes=16 * 1024 * 1024),
        )(*parts)
        return jnp.transpose(offs, (1, 0, 2)), met, cen

    return jax.shard_map(
        per_device,
        mesh=mesh,
        in_specs=(
            P(None, None, ("gx", "gy")),
            P(None, ("gx", "gy")),
            P(None, ("gx", "gy")),
            P(),
            P(),
            P(("gx", "gy"), None, None),
            P(("gx", "gy"), None, None),
            P(("gx", "gy"), None, None),
            P(("gx", "gy"), None),
        ),
        out_specs=(P(None, None, ("gx", "gy")), P(None, ("gx", "gy")), P(None, ("gx", "gy"))),
        check_vma=False,
    )
```

```python
import functools

import jax
import jax.numpy as jnp
from jax import lax
from jax.experimental import pallas as pl
from jax.experimental.pallas import tpu as pltpu
from jax.sharding import PartitionSpec as P

V = 642
NBLK = 6
VB = 107
LANES = 128
CAP = 4
VPAD = 768
HALF = 384
HEADINGS = 8

DIRECTIONS = ((-1, -1), (-1, 0), (-1, 1), (0, -1), (0, 1), (1, -1), (1, 0), (1, 1))
TENSION = 0.5
TIME_STEP = 0.25
FACTOR = 8.0 / VB
LOG2E = 1.4426950408889634
OFF = 1.0e6
MESH = pl.DeviceIdType.MESH
F32 = jnp.float32
BF16 = jnp.bfloat16


def mm(a, b):
    return lax.dot_general(a, b, (((1,), (0,)), ((), ())), preferred_element_type=F32)


def mm_nt(a, b):
    return lax.dot_general(a, b, (((1,), (1,)), ((), ())), preferred_element_type=F32)


def two_pieces(x):
    hi = x.astype(BF16)
    lo = (x - hi.astype(F32)).astype(BF16)
    return hi, lo


def three_pieces(x):
    hi = x.astype(BF16)
    rest = x - hi.astype(F32)
    mid = rest.astype(BF16)
    lo = (rest - mid.astype(F32)).astype(BF16)
    return hi, mid, lo


def id_table(ref, times):
    sub = lax.broadcasted_iota(jnp.int32, (8, LANES), 0) & 3
    tiles = []
    for h in range(HEADINGS):
        tile = jnp.where(
            sub == 0, ref[0, h], jnp.where(sub == 1, ref[1, h], jnp.where(sub == 2, ref[2, h], ref[3, h]))
        )
        tiles += [tile] * times
    return jnp.concatenate(tiles, axis=0)


def kernel(
    n_gx, n_gy,
    x_hbm, met_hbm, cen_hbm, lap_hbm, bend_hbm, mig_hbm, ids_hbm, loc_hbm, cnt_hbm,
    stay_o, come_o, met_come_o, put_o, put_met_o,
    x, met, cen, lap, bend, wide, row_s, row_r, near_s, near_r, cell_s, cell_r, wide2, met_out, met_in,
    bt, qt, w, pp, disp, frame, rel_s, mig_s, ids_s, loc_s, cnt_s, in_sem, send_sem, recv_sem,
):
    gx, gy = lax.axis_index("gx"), lax.axis_index("gy")

    def neighbour(h, sign):
        nth = h + lax.div(h + 4, 8)
        dx, dy = lax.div(nth, 3) - 1, lax.rem(nth, 3) - 1
        return (
            lax.rem(gx + (sign * dx + n_gx), n_gx),
            lax.rem(gy + (sign * dy + n_gy), n_gy),
        )

    barrier = pltpu.get_barrier_semaphore()
    for h in range(HEADINGS):
        pl.semaphore_signal(barrier, inc=1, device_id=neighbour(h, 1), device_id_type=MESH)

    loads = [
        pltpu.make_async_copy(src, dst, in_sem.at[i])
        for i, (src, dst) in enumerate(
            (
                (x_hbm, x), (cen_hbm, cen), (met_hbm, met), (lap_hbm, lap), (bend_hbm, bend),
                (ids_hbm, ids_s), (cnt_hbm, cnt_s), (mig_hbm, mig_s), (loc_hbm, loc_s),
            )
        )
    ]
    for load in loads[5:] + loads[:5]:
        load.start()

    def send(kind, src, dst, h, sign, count=16):
        rows = pl.ds(count * h, count)
        return pltpu.make_async_remote_copy(
            src_ref=src.at[rows],
            dst_ref=dst.at[rows],
            send_sem=send_sem.at[kind, h],
            recv_sem=recv_sem.at[kind, h],
            device_id=neighbour(h, sign),
            device_id_type=MESH,
        )

    row = lax.broadcasted_iota(jnp.int32, (LANES, LANES), 0)
    lane = lax.broadcasted_iota(jnp.int32, (LANES, LANES), 1)
    rk = (row >> 2) & 3
    rj = row & 3

    def spread(one_hot, ks):
        return jnp.concatenate([jnp.where(rk == k, one_hot, 0.0) for k in ks], axis=1)

    for load in loads[5:]:
        load.wait()
    ids = id_table(ids_s, 2)
    owner = (ids * 10923) >> 16
    block = ids - NBLK * owner
    own_hot = (lane == owner).astype(F32)
    loc_hot = (lane == id_table(loc_s, 2)).astype(F32)

    def rows_lanes(rows):
        shape = (rows, LANES)
        return lax.broadcasted_iota(jnp.int32, shape, 0), lax.broadcasted_iota(jnp.int32, shape, 1)

    row64, lane64 = rows_lanes(64)
    row192, lane192 = rows_lanes(192)
    late64 = (row64 & 4) == 4
    late192 = (row192 & 4) == 4
    tile192 = row192 >> 3
    k192 = tile192 - 3 * ((tile192 * 171) >> 9)
    met_hot = (lane64 == id_table(mig_s, 1)).astype(F32)
    mig_hot = (lane192 == id_table(mig_s, 3)).astype(F32)

    def halves(full, late):
        late3 = jnp.concatenate([late, late, late], axis=1)
        return jnp.where(late3, full[:, HALF:], full[:, :HALF])

    counts = jnp.concatenate(
        [jnp.full((16, LANES), cnt_s[0, h], jnp.int32) for h in range(HEADINGS)], axis=0
    )
    live = (rj < counts) & (lane < VB)

    loads[0].wait()
    loads[1].wait()
    x0, x1, x2 = x[0], x[1], x[2]
    xcat = jnp.concatenate([x0, x1, x2], axis=1)
    cen_rows = jnp.where(rk == 0, cen[0:1, :], jnp.where(rk == 1, cen[1:2, :], cen[2:3, :]))
    cen_rows = jnp.where(rk == 3, 0.0, cen_rows)
    wide[:, VPAD - LANES:] = jnp.zeros((LANES, LANES), F32)
    wide[:, :V] = mm_nt(spread(own_hot, (0, 1, 2)).astype(BF16), xcat)
    picked = jnp.zeros((LANES, LANES), F32)
    for b in range(NBLK):
        tile, shift = divmod(VB * b, LANES)
        two = wide[:, tile * LANES:(tile + 2) * LANES]
        if shift:
            two = pltpu.roll(two, 2 * LANES - shift, 1)
        picked = jnp.where(block == b, two[:, :LANES], picked)
    own_cen = jnp.sum(own_hot * cen_rows, axis=1, keepdims=True)
    row_s[...] = jnp.where(live, jnp.where(rk == 3, 1.0, picked + own_cen), 0.0)

    pl.semaphore_wait(barrier, HEADINGS)
    row_sends = [send(0, row_s, row_r, h, 1) for h in range(HEADINGS)]
    for copy in row_sends:
        copy.start()

    loads[2].wait()
    metric = met[...]
    wide2[:, VPAD - LANES:] = jnp.zeros((192, LANES), F32)
    wide2[:64, :V] = mm_nt(met_hot.astype(BF16), metric)
    met_out[...] = halves(wide2[:64, :], late64)
    metric_sends = [send(3, met_out, met_in, h, 1, 8) for h in range(HEADINGS)]
    for copy in metric_sends:
        copy.start()

    loc_spread = spread(loc_hot, (0, 1, 2)).astype(BF16)
    f0, f1, f2 = x0.astype(F32), x1.astype(F32), x2.astype(F32)
    sq = (f0 * f0 + f1 * f1 + f2 * f2) * (-0.25 * LOG2E)
    source = jnp.concatenate([x0, x1, x2, *three_pieces(sq)], axis=1)
    none = jnp.zeros((LANES, 3 * LANES), BF16)
    take_q = jnp.concatenate([loc_spread, none], axis=1)
    take_sq = jnp.concatenate([none, loc_spread], axis=1)
    parts = []
    for h in range(HEADINGS):
        rows = slice(16 * h, 16 * h + 16)
        parts += [take_q[rows], take_q[rows], take_q[rows], take_sq[rows]]
    take = jnp.concatenate(parts, axis=0)
    col = lax.broadcasted_iota(jnp.int32, (1, 512), 1)
    ones_col = jnp.where((((col >> 4) & 3) < 3) & (((col >> 2) & 3) == 3), 1.0, 0.0)
    bt[...] = (mm_nt(source, take) + ones_col).astype(BF16)
    ones_row = jnp.where(rk == 3, 1.0, 0.0)[:, :1]
    qt[...] = (mm_nt(loc_spread, xcat) + ones_row).astype(BF16)
    frame[...] = jnp.broadcast_to(jnp.sum(loc_hot * cen_rows, axis=1, keepdims=True), (LANES, LANES))

    loads[3].wait()
    loads[4].wait()
    m1 = metric.astype(F32)
    m3 = jnp.concatenate([m1, m1, m1], axis=1)
    curvature = mm(lap[...], xcat)
    weighted = (m3 * curvature).astype(BF16)
    force = m3 * (TENSION * curvature - mm(lap[...], weighted)) - mm(bend[...], xcat)
    cen3 = jnp.concatenate([cen[0:1, :], cen[1:2, :], cen[2:3, :]], axis=1)
    xf = jnp.concatenate([f0, f1, f2], axis=1)
    disp[...] = xf + cen3 + TIME_STEP * force

    one16 = jnp.ones((16, LANES), BF16)
    row32, rk32 = row[:32], rk[:32]
    rj16 = rj[:16]
    backwards = lax.rem(gx + 1, n_gx // 2) == 0
    near_sends = []
    for step in range(4):
        t = jnp.where(backwards, 3 - step, step)
        for i in range(2):
            send(0, row_s, row_r, 2 * t + i, 1).wait_recv()
        rows = pl.ds(pl.multiple_of(32 * t, 32), 32)
        got = row_r[rows, :]
        rel = got - frame[rows, :]
        rel_s[rows, :] = rel
        rel_sq = jnp.where(rk32 == 3, 0.0, rel * rel)
        tot = pltpu.roll(rel_sq, 4, 0) + pltpu.roll(rel_sq, 8, 0) + pltpu.roll(rel_sq, 12, 0)
        vals = jnp.where(
            rk32 == 3, (-0.25 * LOG2E) * tot - OFF * (1.0 - got), (0.5 * LOG2E) * rel
        )
        v0, v1, v2 = three_pieces(vals)
        base = jnp.concatenate(
            [v0[:16], v1[:16], v2[:16], one16, v0[16:], v1[16:], v2[16:], one16], axis=0
        )
        left = bt[:, pl.ds(pl.multiple_of(t * LANES, LANES), LANES)]
        weights = []
        for q in range(4):
            right = jnp.concatenate(
                [
                    jnp.where(((row >> 6) == (q // 2)) & (rj == 2 * (q % 2) + i), base, jnp.zeros_like(base))
                    for i in range(2)
                ],
                axis=1,
            )
            pair = jnp.exp2(mm(left, right)).astype(BF16)
            w[:, pl.ds(pl.multiple_of(1024 * t + 256 * q, 256), 256)] = pair
            weights.append(pair)
        sums = []
        for i in range(2):
            mine = None
            partner = qt[pl.ds(pl.multiple_of(32 * t + 16 * i, 16), 16), :]
            for j2 in range(2):
                two = mm(partner, weights[2 * i + j2])
                for j in range(2):
                    part = two[:, j * LANES:(j + 1) * LANES]
                    mine = part if mine is None else jnp.where(rj16 == 2 * j2 + j, part, mine)
            sums.append(mine)
        total = jnp.concatenate(sums, axis=0)
        weight = jnp.where(
            rk32 == 0,
            pltpu.roll(total, 20, 0),
            jnp.where(rk32 == 1, pltpu.roll(total, 24, 0), pltpu.roll(total, 28, 0)),
        )
        near_s[rows, :] = FACTOR * (rel * weight - total)
        for i in range(2):
            copy = send(1, near_s, near_r, 2 * t + i, -1)
            copy.start()
            near_sends.append(copy)
    for copy in row_sends:
        copy.wait_send()

    rel_t = jnp.transpose(jnp.where(rk == 3, 1.0, rel_s[...]))
    rel_hi, rel_lo = two_pieces(rel_t)
    rel2 = jnp.concatenate([rel_hi, rel_lo], axis=1)
    lane2 = lax.broadcasted_iota(jnp.int32, (LANES, 2 * LANES), 1) & 127
    for h in range(HEADINGS):
        for j in range(CAP):
            at = (4 * h + j) * LANES
            pp[at:at + LANES, :] = jnp.where(
                ((lane2 >> 4) == h) & ((lane2 & 3) == j), rel2, jnp.zeros_like(rel2)
            )
    far2 = mm(w[...], pp[...])
    far = jnp.concatenate(two_pieces(far2[:, :LANES] + far2[:, LANES:]), axis=1)
    loc_put = spread(loc_hot, (0, 1, 2, 3)).astype(BF16)
    put = mm(far, jnp.concatenate([loc_put, loc_put], axis=0))
    put3 = put[:, 3 * LANES:]
    weight3 = jnp.concatenate([put3, put3, put3], axis=1)
    disp[...] = disp[...] - (TIME_STEP * FACTOR) * (put[:, :3 * LANES] - xf * weight3)

    pick3 = jnp.concatenate([jnp.where(k192 == k, mig_hot, 0.0) for k in range(3)], axis=1).astype(BF16)
    pick = jnp.concatenate([pick3, pick3], axis=1)
    wide2[:, :V] = mm_nt(pick, jnp.concatenate(two_pieces(disp[...]), axis=1))
    leave = halves(wide2[...], late192)
    own_spread = spread(own_hot, (0, 1, 2))
    own_b16 = own_spread.astype(BF16)
    same = (TIME_STEP * mm_nt(pick3, own_b16)).astype(BF16)
    same = jnp.concatenate([same, same], axis=1)
    block3 = jnp.concatenate([block, block, block], axis=1)
    near_put = jnp.concatenate(
        [jnp.where(block3 == b, own_spread, 0.0).astype(BF16) for b in range(NBLK)], axis=1
    )
    near_put = jnp.concatenate([near_put, near_put], axis=0)

    for copy in near_sends:
        copy.wait()
    near = jnp.where(rk == 3, 0.0, near_r[...])
    places = [jnp.zeros((LANES, LANES), F32) for _ in range(VPAD // LANES)]
    for b in range(NBLK):
        tile, shift = divmod(VB * b, LANES)
        piece = jnp.where((block == b) & (lane < VB), near, 0.0)
        if shift:
            piece = pltpu.roll(piece, shift, 1)
            places[tile + 1] = places[tile + 1] + jnp.where(lane < shift, piece, 0.0)
            piece = jnp.where(lane >= shift, piece, 0.0)
        places[tile] = places[tile] + piece
    placed = jnp.concatenate(places, axis=1)
    cell_s[...] = leave + halves(mm(same, jnp.concatenate(two_pieces(placed), axis=0)), late192)
    cell_sends = [send(2, cell_s, cell_r, h, 1, 24) for h in range(HEADINGS)]
    for copy in cell_sends:
        copy.start()

    near_t = jnp.concatenate(two_pieces(jnp.transpose(near)), axis=1)
    back = mm(near_t, near_put)
    for b in range(NBLK):
        rows = slice(VB * b, VB * b + VB)
        disp[rows, :] = disp[rows, :] + TIME_STEP * back[:VB, 384 * b:384 * b + 384]
    keep = 1.0 - jnp.sum(jnp.where(late64, 0.0, met_hot), axis=0, keepdims=True)
    keep3 = jnp.concatenate([keep, keep, keep], axis=1)
    stay_o[:, :3 * LANES] = disp[...] * keep3
    stay_o[:, 3 * LANES:] = m1 * keep
    late3 = jnp.concatenate([late192, late192, late192], axis=1)
    for half in range(2):
        put = jnp.where(late3 == (half == 1), pick3, jnp.zeros_like(pick3))
        put_o[half] = jnp.concatenate([put, put], axis=0)
        put_met_o[half] = jnp.where(late64 == (half == 1), met_hot, 0.0).astype(BF16)
    for copy in metric_sends:
        copy.wait()
    met_come_o[...] = met_in[...]
    for copy in cell_sends:
        copy.wait()
    come_o[...] = cell_r[...]


def settle(stay, come, met_come, put, put_met, off_hbm, met_hbm, cen_hbm, off, met, cen, sem):
    met_cells = jnp.transpose(met_come[...]).astype(BF16)
    met_in = jnp.concatenate([mm(met_cells, put_met[0]), mm(met_cells, put_met[1])], axis=0)[:V]
    met[...] = (stay[:, 3 * LANES:] + met_in).astype(BF16)
    copies = [pltpu.make_async_copy(met, met_hbm, sem.at[0])]
    copies[0].start()
    cells = jnp.concatenate(two_pieces(jnp.transpose(come[...])), axis=1)
    for k in range(3):
        lanes = slice(k * LANES, (k + 1) * LANES)
        arrived = jnp.concatenate([mm(cells, put[0][:, lanes]), mm(cells, put[1][:, lanes])], axis=0)[:V]
        settled = stay[:, lanes] + arrived
        centre = jnp.sum(settled, axis=0, keepdims=True) * (1.0 / V)
        off[k] = (settled - centre).astype(BF16)
        cen[k:k + 1, :] = centre
        copies.append(pltpu.make_async_copy(off.at[k], off_hbm.at[k], sem.at[k + 1]))
        copies[-1].start()
    copies.append(pltpu.make_async_copy(cen, cen_hbm, sem.at[4]))
    copies[-1].start()
    for copy in copies:
        copy.wait()


def solution(mesh):
    n_gx, n_gy = mesh.shape["gx"], mesh.shape["gy"]

    def per_device(offsets, metric, centers, lap, bend, mig_slots, contact_ids, contact_local, contact_count):
        hbm = pl.BlockSpec(memory_space=pltpu.HBM)
        vmem = pl.BlockSpec(memory_space=pltpu.VMEM)
        parts = pl.pallas_call(
            functools.partial(kernel, n_gx, n_gy),
            out_shape=(
                pltpu.VMEM((V, 4 * LANES), F32),
                pltpu.VMEM((192, HALF), F32),
                pltpu.VMEM((64, HALF), F32),
                pltpu.VMEM((2, HALF, 3 * LANES), BF16),
                pltpu.VMEM((2, 64, LANES), BF16),
            ),
            in_specs=[hbm] * 9,
            out_specs=(vmem,) * 5,
            scratch_shapes=[
                pltpu.VMEM((3, V, LANES), BF16),
                pltpu.VMEM((V, LANES), BF16),
                pltpu.VMEM((3, LANES), F32),
                pltpu.VMEM((V, V), BF16),
                pltpu.VMEM((V, V), BF16),
                pltpu.VMEM((LANES, VPAD), F32),
                pltpu.VMEM((LANES, LANES), F32),
                pltpu.VMEM((LANES, LANES), F32),
                pltpu.VMEM((LANES, LANES), F32),
                pltpu.VMEM((LANES, LANES), F32),
                pltpu.VMEM((192, HALF), F32),
                pltpu.VMEM((192, HALF), F32),
                pltpu.VMEM((192, VPAD), F32),
                pltpu.VMEM((64, HALF), F32),
                pltpu.VMEM((64, HALF), F32),
                pltpu.VMEM((V, 512), BF16),
                pltpu.VMEM((LANES, V), BF16),
                pltpu.VMEM((V, 32 * LANES), BF16),
                pltpu.VMEM((32 * LANES, 2 * LANES), BF16),
                pltpu.VMEM((V, 3 * LANES), F32),
                pltpu.VMEM((LANES, LANES), F32),
                pltpu.VMEM((LANES, LANES), F32),
                pltpu.SMEM((CAP, HEADINGS), jnp.int32),
                pltpu.SMEM((CAP, HEADINGS), jnp.int32),
                pltpu.SMEM((CAP, HEADINGS), jnp.int32),
                pltpu.SMEM((1, HEADINGS), jnp.int32),
                pltpu.SemaphoreType.DMA((9,)),
                pltpu.SemaphoreType.DMA((4, HEADINGS)),
                pltpu.SemaphoreType.DMA((4, HEADINGS)),
            ],
            compiler_params=pltpu.CompilerParams(
                collective_id=0, has_side_effects=True, vmem_limit_bytes=58 * 1024 * 1024
            ),
        )(
            jnp.transpose(offsets, (1, 0, 2)),
            metric,
            centers,
            lap,
            bend,
            jnp.transpose(mig_slots[0]),
            jnp.transpose(contact_ids[0]),
            jnp.transpose(contact_local[0]),
            contact_count,
        )
        offs, met, cen = pl.pallas_call(
            settle,
            out_shape=(
                jax.ShapeDtypeStruct((3, V, LANES), BF16),
                jax.ShapeDtypeStruct((V, LANES), BF16),
                jax.ShapeDtypeStruct((3, LANES), F32),
            ),
            in_specs=[vmem] * 5,
            out_specs=(hbm, hbm, hbm),
            scratch_shapes=[
                pltpu.VMEM((3, V, LANES), BF16),
                pltpu.VMEM((V, LANES), BF16),
                pltpu.VMEM((3, LANES), F32),
                pltpu.SemaphoreType.DMA((5,)),
            ],
            compiler_params=pltpu.CompilerParams(vmem_limit_bytes=16 * 1024 * 1024),
        )(*parts)
        return jnp.transpose(offs, (1, 0, 2)), met, cen

    return jax.shard_map(
        per_device,
        mesh=mesh,
        in_specs=(
            P(None, None, ("gx", "gy")),
            P(None, ("gx", "gy")),
            P(None, ("gx", "gy")),
            P(),
            P(),
            P(("gx", "gy"), None, None),
            P(("gx", "gy"), None, None),
            P(("gx", "gy"), None, None),
            P(("gx", "gy"), None),
        ),
        out_specs=(P(None, None, ("gx", "gy")), P(None, ("gx", "gy")), P(None, ("gx", "gy"))),
        check_vma=False,
    )
```

```python
import functools

import jax
import jax.numpy as jnp
from jax import lax
from jax.experimental import pallas as pl
from jax.experimental.pallas import tpu as pltpu
from jax.sharding import PartitionSpec as P

V = 642
NBLK = 6
VB = 107
LANES = 128
CAP = 4
VPAD = 768
HALF = 384
HEADINGS = 8

DIRECTIONS = ((-1, -1), (-1, 0), (-1, 1), (0, -1), (0, 1), (1, -1), (1, 0), (1, 1))
TENSION = 0.5
TIME_STEP = 0.25
FACTOR = 8.0 / VB
LOG2E = 1.4426950408889634
OFF = 1.0e6
MESH = pl.DeviceIdType.MESH
F32 = jnp.float32
BF16 = jnp.bfloat16


def mm(a, b):
    return lax.dot_general(a, b, (((1,), (0,)), ((), ())), preferred_element_type=F32)


def mm_nt(a, b):
    return lax.dot_general(a, b, (((1,), (1,)), ((), ())), preferred_element_type=F32)


def two_pieces(x):
    hi = x.astype(BF16)
    lo = (x - hi.astype(F32)).astype(BF16)
    return hi, lo


def three_pieces(x):
    hi = x.astype(BF16)
    rest = x - hi.astype(F32)
    mid = rest.astype(BF16)
    lo = (rest - mid.astype(F32)).astype(BF16)
    return hi, mid, lo


def id_table(ref, times):
    sub = lax.broadcasted_iota(jnp.int32, (8, LANES), 0) & 3
    tiles = []
    for h in range(HEADINGS):
        tile = jnp.where(
            sub == 0, ref[0, h], jnp.where(sub == 1, ref[1, h], jnp.where(sub == 2, ref[2, h], ref[3, h]))
        )
        tiles += [tile] * times
    return jnp.concatenate(tiles, axis=0)


def kernel(
    n_gx, n_gy,
    x_hbm, met_hbm, cen_hbm, lap_hbm, bend_hbm, mig_hbm, ids_hbm, loc_hbm, cnt_hbm,
    stay_o, come_o, met_come_o, put_o, put_met_o,
    x, met, cen, lap, bend, wide, row_s, row_r, near_s, near_r, cell_s, cell_r, wide2, met_out, met_in,
    bt, qt, w, pp, disp, frame, rel_s, mig_s, ids_s, loc_s, cnt_s, in_sem, send_sem, recv_sem,
):
    gx, gy = lax.axis_index("gx"), lax.axis_index("gy")

    def neighbour(h, sign):
        nth = h + lax.div(h + 4, 8)
        dx, dy = lax.div(nth, 3) - 1, lax.rem(nth, 3) - 1
        return (
            lax.rem(gx + (sign * dx + n_gx), n_gx),
            lax.rem(gy + (sign * dy + n_gy), n_gy),
        )

    barrier = pltpu.get_barrier_semaphore()
    for h in range(HEADINGS):
        pl.semaphore_signal(barrier, inc=1, device_id=neighbour(h, 1), device_id_type=MESH)

    loads = [
        pltpu.make_async_copy(src, dst, in_sem.at[i])
        for i, (src, dst) in enumerate(
            (
                (x_hbm, x), (cen_hbm, cen), (met_hbm, met), (lap_hbm, lap), (bend_hbm, bend),
                (ids_hbm, ids_s), (cnt_hbm, cnt_s), (mig_hbm, mig_s), (loc_hbm, loc_s),
            )
        )
    ]
    for load in loads[5:] + loads[:5]:
        load.start()

    def send(kind, src, dst, h, sign, count=16):
        rows = pl.ds(count * h, count)
        return pltpu.make_async_remote_copy(
            src_ref=src.at[rows],
            dst_ref=dst.at[rows],
            send_sem=send_sem.at[kind, h],
            recv_sem=recv_sem.at[kind, h],
            device_id=neighbour(h, sign),
            device_id_type=MESH,
        )

    row = lax.broadcasted_iota(jnp.int32, (LANES, LANES), 0)
    lane = lax.broadcasted_iota(jnp.int32, (LANES, LANES), 1)
    rk = (row >> 2) & 3
    rj = row & 3

    def spread(one_hot, ks):
        return jnp.concatenate([jnp.where(rk == k, one_hot, 0.0) for k in ks], axis=1)

    for load in loads[5:]:
        load.wait()
    ids = id_table(ids_s, 2)
    owner = (ids * 10923) >> 16
    block = ids - NBLK * owner
    own_hot = (lane == owner).astype(F32)
    loc_hot = (lane == id_table(loc_s, 2)).astype(F32)

    def rows_lanes(rows):
        shape = (rows, LANES)
        return lax.broadcasted_iota(jnp.int32, shape, 0), lax.broadcasted_iota(jnp.int32, shape, 1)

    row64, lane64 = rows_lanes(64)
    row192, lane192 = rows_lanes(192)
    late64 = (row64 & 4) == 4
    late192 = (row192 & 4) == 4
    tile192 = row192 >> 3
    k192 = tile192 - 3 * ((tile192 * 171) >> 9)
    met_hot = (lane64 == id_table(mig_s, 1)).astype(F32)
    mig_hot = (lane192 == id_table(mig_s, 3)).astype(F32)

    def halves(full, late):
        late3 = jnp.concatenate([late, late, late], axis=1)
        return jnp.where(late3, full[:, HALF:], full[:, :HALF])

    counts = jnp.concatenate(
        [jnp.full((16, LANES), cnt_s[0, h], jnp.int32) for h in range(HEADINGS)], axis=0
    )
    live = (rj < counts) & (lane < VB)

    loads[0].wait()
    loads[1].wait()
    x0, x1, x2 = x[0], x[1], x[2]
    xcat = jnp.concatenate([x0, x1, x2], axis=1)
    cen_rows = jnp.where(rk == 0, cen[0:1, :], jnp.where(rk == 1, cen[1:2, :], cen[2:3, :]))
    cen_rows = jnp.where(rk == 3, 0.0, cen_rows)
    wide[:, VPAD - LANES:] = jnp.zeros((LANES, LANES), F32)
    wide[:, :V] = mm_nt(spread(own_hot, (0, 1, 2)).astype(BF16), xcat)
    picked = jnp.zeros((LANES, LANES), F32)
    for b in range(NBLK):
        tile, shift = divmod(VB * b, LANES)
        two = wide[:, tile * LANES:(tile + 2) * LANES]
        if shift:
            two = pltpu.roll(two, 2 * LANES - shift, 1)
        picked = jnp.where(block == b, two[:, :LANES], picked)
    own_cen = jnp.sum(own_hot * cen_rows, axis=1, keepdims=True)
    row_s[...] = jnp.where(live, jnp.where(rk == 3, 1.0, picked + own_cen), 0.0)

    pl.semaphore_wait(barrier, HEADINGS)
    row_sends = [send(0, row_s, row_r, h, 1) for h in range(HEADINGS)]
    for copy in row_sends:
        copy.start()

    loads[2].wait()
    metric = met[...]
    wide2[:, VPAD - LANES:] = jnp.zeros((192, LANES), F32)
    wide2[:64, :V] = mm_nt(met_hot.astype(BF16), metric)
    met_out[...] = halves(wide2[:64, :], late64)
    metric_sends = [send(3, met_out, met_in, h, 1, 8) for h in range(HEADINGS)]
    for copy in metric_sends:
        copy.start()

    loc_spread = spread(loc_hot, (0, 1, 2)).astype(BF16)
    f0, f1, f2 = x0.astype(F32), x1.astype(F32), x2.astype(F32)
    sq = (f0 * f0 + f1 * f1 + f2 * f2) * (-0.25 * LOG2E)
    source = jnp.concatenate([x0, x1, x2, *three_pieces(sq)], axis=1)
    none = jnp.zeros((LANES, 3 * LANES), BF16)
    take_q = jnp.concatenate([loc_spread, none], axis=1)
    take_sq = jnp.concatenate([none, loc_spread], axis=1)
    parts = []
    for h in range(HEADINGS):
        rows = slice(16 * h, 16 * h + 16)
        parts += [take_q[rows], take_q[rows], take_q[rows], take_sq[rows]]
    take = jnp.concatenate(parts, axis=0)
    col = lax.broadcasted_iota(jnp.int32, (1, 512), 1)
    ones_col = jnp.where((((col >> 4) & 3) < 3) & (((col >> 2) & 3) == 3), 1.0, 0.0)
    bt[...] = (mm_nt(source, take) + ones_col).astype(BF16)
    ones_row = jnp.where(rk == 3, 1.0, 0.0)[:, :1]
    qt[...] = (mm_nt(loc_spread, xcat) + ones_row).astype(BF16)
    frame[...] = jnp.broadcast_to(jnp.sum(loc_hot * cen_rows, axis=1, keepdims=True), (LANES, LANES))

    loads[3].wait()
    loads[4].wait()
    m1 = metric.astype(F32)
    m3 = jnp.concatenate([m1, m1, m1], axis=1)
    curvature = mm(lap[...], xcat)
    weighted = (m3 * curvature).astype(BF16)
    force = m3 * (TENSION * curvature - mm(lap[...], weighted)) - mm(bend[...], xcat)
    cen3 = jnp.concatenate([cen[0:1, :], cen[1:2, :], cen[2:3, :]], axis=1)
    xf = jnp.concatenate([f0, f1, f2], axis=1)
    disp[...] = xf + cen3 + TIME_STEP * force

    one16 = jnp.ones((16, LANES), BF16)
    row32, rk32 = row[:32], rk[:32]
    rj16 = rj[:16]
    backwards = lax.rem(gx + 1, n_gx // 2) == 0
    near_sends = []
    for step in range(4):
        t = jnp.where(backwards, 3 - step, step)
        for i in range(2):
            send(0, row_s, row_r, 2 * t + i, 1).wait_recv()
        rows = pl.ds(pl.multiple_of(32 * t, 32), 32)
        got = row_r[rows, :]
        rel = got - frame[rows, :]
        rel_s[rows, :] = rel
        rel_sq = jnp.where(rk32 == 3, 0.0, rel * rel)
        tot = pltpu.roll(rel_sq, 4, 0) + pltpu.roll(rel_sq, 8, 0) + pltpu.roll(rel_sq, 12, 0)
        vals = jnp.where(
            rk32 == 3, (-0.25 * LOG2E) * tot - OFF * (1.0 - got), (0.5 * LOG2E) * rel
        )
        v0, v1, v2 = three_pieces(vals)
        base = jnp.concatenate(
            [v0[:16], v1[:16], v2[:16], one16, v0[16:], v1[16:], v2[16:], one16], axis=0
        )
        left = bt[:, pl.ds(pl.multiple_of(t * LANES, LANES), LANES)]
        weights = []
        for q in range(4):
            right = jnp.concatenate(
                [
                    jnp.where(((row >> 6) == (q // 2)) & (rj == 2 * (q % 2) + i), base, jnp.zeros_like(base))
                    for i in range(2)
                ],
                axis=1,
            )
            pair = jnp.exp2(mm(left, right)).astype(BF16)
            w[:, pl.ds(pl.multiple_of(1024 * t + 256 * q, 256), 256)] = pair
            weights.append(pair)
        sums = []
        for i in range(2):
            mine = None
            partner = qt[pl.ds(pl.multiple_of(32 * t + 16 * i, 16), 16), :]
            for j2 in range(2):
                two = mm(partner, weights[2 * i + j2])
                for j in range(2):
                    part = two[:, j * LANES:(j + 1) * LANES]
                    mine = part if mine is None else jnp.where(rj16 == 2 * j2 + j, part, mine)
            sums.append(mine)
        total = jnp.concatenate(sums, axis=0)
        weight = jnp.where(
            rk32 == 0,
            pltpu.roll(total, 20, 0),
            jnp.where(rk32 == 1, pltpu.roll(total, 24, 0), pltpu.roll(total, 28, 0)),
        )
        near_s[rows, :] = FACTOR * (rel * weight - total)
        for i in range(2):
            copy = send(1, near_s, near_r, 2 * t + i, -1)
            copy.start()
            near_sends.append(copy)

    rel_t = jnp.transpose(jnp.where(rk == 3, 1.0, rel_s[...]))
    rel_hi, rel_lo = two_pieces(rel_t)
    rel2 = jnp.concatenate([rel_hi, rel_lo], axis=1)
    lane2 = lax.broadcasted_iota(jnp.int32, (LANES, 2 * LANES), 1) & 127
    for h in range(HEADINGS):
        for j in range(CAP):
            at = (4 * h + j) * LANES
            pp[at:at + LANES, :] = jnp.where(
                ((lane2 >> 4) == h) & ((lane2 & 3) == j), rel2, jnp.zeros_like(rel2)
            )
    far2 = mm(w[...], pp[...])
    far = jnp.concatenate(two_pieces(far2[:, :LANES] + far2[:, LANES:]), axis=1)
    loc_put = spread(loc_hot, (0, 1, 2, 3)).astype(BF16)
    put = mm(far, jnp.concatenate([loc_put, loc_put], axis=0))
    put3 = put[:, 3 * LANES:]
    weight3 = jnp.concatenate([put3, put3, put3], axis=1)
    disp[...] = disp[...] - (TIME_STEP * FACTOR) * (put[:, :3 * LANES] - xf * weight3)

    pick3 = jnp.concatenate([jnp.where(k192 == k, mig_hot, 0.0) for k in range(3)], axis=1).astype(BF16)
    pick = jnp.concatenate([pick3, pick3], axis=1)
    wide2[:, :V] = mm_nt(pick, jnp.concatenate(two_pieces(disp[...]), axis=1))
    leave = halves(wide2[...], late192)
    own_spread = spread(own_hot, (0, 1, 2))
    own_b16 = own_spread.astype(BF16)
    same = (TIME_STEP * mm_nt(pick3, own_b16)).astype(BF16)
    same = jnp.concatenate([same, same], axis=1)
    block3 = jnp.concatenate([block, block, block], axis=1)
    near_put = jnp.concatenate(
        [jnp.where(block3 == b, own_spread, 0.0).astype(BF16) for b in range(NBLK)], axis=1
    )
    near_put = jnp.concatenate([near_put, near_put], axis=0)

    for copy in near_sends:
        copy.wait_recv()
    near = jnp.where(rk == 3, 0.0, near_r[...])
    places = [jnp.zeros((LANES, LANES), F32) for _ in range(VPAD // LANES)]
    for b in range(NBLK):
        tile, shift = divmod(VB * b, LANES)
        piece = jnp.where((block == b) & (lane < VB), near, 0.0)
        if shift:
            piece = pltpu.roll(piece, shift, 1)
            places[tile + 1] = places[tile + 1] + jnp.where(lane < shift, piece, 0.0)
            piece = jnp.where(lane >= shift, piece, 0.0)
        places[tile] = places[tile] + piece
    placed = jnp.concatenate(places, axis=1)
    cell_s[...] = leave + halves(mm(same, jnp.concatenate(two_pieces(placed), axis=0)), late192)
    cell_sends = [send(2, cell_s, cell_r, h, 1, 24) for h in range(HEADINGS)]
    for copy in cell_sends:
        copy.start()

    near_t = jnp.concatenate(two_pieces(jnp.transpose(near)), axis=1)
    back = mm(near_t, near_put)
    for b in range(NBLK):
        rows = slice(VB * b, VB * b + VB)
        disp[rows, :] = disp[rows, :] + TIME_STEP * back[:VB, 384 * b:384 * b + 384]
    keep = 1.0 - jnp.sum(jnp.where(late64, 0.0, met_hot), axis=0, keepdims=True)
    keep3 = jnp.concatenate([keep, keep, keep], axis=1)
    stay_o[:, :3 * LANES] = disp[...] * keep3
    stay_o[:, 3 * LANES:] = m1 * keep
    late3 = jnp.concatenate([late192, late192, late192], axis=1)
    for half in range(2):
        put = jnp.where(late3 == (half == 1), pick3, jnp.zeros_like(pick3))
        put_o[half] = jnp.concatenate([put, put], axis=0)
        put_met_o[half] = jnp.where(late64 == (half == 1), met_hot, 0.0).astype(BF16)
    for copy in metric_sends:
        copy.wait()
    met_come_o[...] = met_in[...]
    for copy in row_sends + near_sends:
        copy.wait_send()
    for copy in cell_sends:
        copy.wait()
    come_o[...] = cell_r[...]


def settle(stay, come, met_come, put, put_met, off_hbm, met_hbm, cen_hbm, off, met, cen, sem):
    met_cells = jnp.transpose(met_come[...]).astype(BF16)
    met_in = jnp.concatenate([mm(met_cells, put_met[0]), mm(met_cells, put_met[1])], axis=0)[:V]
    met[...] = (stay[:, 3 * LANES:] + met_in).astype(BF16)
    copies = [pltpu.make_async_copy(met, met_hbm, sem.at[0])]
    copies[0].start()
    cells = jnp.concatenate(two_pieces(jnp.transpose(come[...])), axis=1)
    for k in range(3):
        lanes = slice(k * LANES, (k + 1) * LANES)
        arrived = jnp.concatenate([mm(cells, put[0][:, lanes]), mm(cells, put[1][:, lanes])], axis=0)[:V]
        settled = stay[:, lanes] + arrived
        centre = jnp.sum(settled, axis=0, keepdims=True) * (1.0 / V)
        off[k] = (settled - centre).astype(BF16)
        cen[k:k + 1, :] = centre
        copies.append(pltpu.make_async_copy(off.at[k], off_hbm.at[k], sem.at[k + 1]))
        copies[-1].start()
    copies.append(pltpu.make_async_copy(cen, cen_hbm, sem.at[4]))
    copies[-1].start()
    for copy in copies:
        copy.wait()


def solution(mesh):
    n_gx, n_gy = mesh.shape["gx"], mesh.shape["gy"]

    def per_device(offsets, metric, centers, lap, bend, mig_slots, contact_ids, contact_local, contact_count):
        hbm = pl.BlockSpec(memory_space=pltpu.HBM)
        vmem = pl.BlockSpec(memory_space=pltpu.VMEM)
        parts = pl.pallas_call(
            functools.partial(kernel, n_gx, n_gy),
            out_shape=(
                pltpu.VMEM((V, 4 * LANES), F32),
                pltpu.VMEM((192, HALF), F32),
                pltpu.VMEM((64, HALF), F32),
                pltpu.VMEM((2, HALF, 3 * LANES), BF16),
                pltpu.VMEM((2, 64, LANES), BF16),
            ),
            in_specs=[hbm] * 9,
            out_specs=(vmem,) * 5,
            scratch_shapes=[
                pltpu.VMEM((3, V, LANES), BF16),
                pltpu.VMEM((V, LANES), BF16),
                pltpu.VMEM((3, LANES), F32),
                pltpu.VMEM((V, V), BF16),
                pltpu.VMEM((V, V), BF16),
                pltpu.VMEM((LANES, VPAD), F32),
                pltpu.VMEM((LANES, LANES), F32),
                pltpu.VMEM((LANES, LANES), F32),
                pltpu.VMEM((LANES, LANES), F32),
                pltpu.VMEM((LANES, LANES), F32),
                pltpu.VMEM((192, HALF), F32),
                pltpu.VMEM((192, HALF), F32),
                pltpu.VMEM((192, VPAD), F32),
                pltpu.VMEM((64, HALF), F32),
                pltpu.VMEM((64, HALF), F32),
                pltpu.VMEM((V, 512), BF16),
                pltpu.VMEM((LANES, V), BF16),
                pltpu.VMEM((V, 32 * LANES), BF16),
                pltpu.VMEM((32 * LANES, 2 * LANES), BF16),
                pltpu.VMEM((V, 3 * LANES), F32),
                pltpu.VMEM((LANES, LANES), F32),
                pltpu.VMEM((LANES, LANES), F32),
                pltpu.SMEM((CAP, HEADINGS), jnp.int32),
                pltpu.SMEM((CAP, HEADINGS), jnp.int32),
                pltpu.SMEM((CAP, HEADINGS), jnp.int32),
                pltpu.SMEM((1, HEADINGS), jnp.int32),
                pltpu.SemaphoreType.DMA((9,)),
                pltpu.SemaphoreType.DMA((4, HEADINGS)),
                pltpu.SemaphoreType.DMA((4, HEADINGS)),
            ],
            compiler_params=pltpu.CompilerParams(
                collective_id=0, has_side_effects=True, vmem_limit_bytes=58 * 1024 * 1024
            ),
        )(
            jnp.transpose(offsets, (1, 0, 2)),
            metric,
            centers,
            lap,
            bend,
            jnp.transpose(mig_slots[0]),
            jnp.transpose(contact_ids[0]),
            jnp.transpose(contact_local[0]),
            contact_count,
        )
        offs, met, cen = pl.pallas_call(
            settle,
            out_shape=(
                jax.ShapeDtypeStruct((3, V, LANES), BF16),
                jax.ShapeDtypeStruct((V, LANES), BF16),
                jax.ShapeDtypeStruct((3, LANES), F32),
            ),
            in_specs=[vmem] * 5,
            out_specs=(hbm, hbm, hbm),
            scratch_shapes=[
                pltpu.VMEM((3, V, LANES), BF16),
                pltpu.VMEM((V, LANES), BF16),
                pltpu.VMEM((3, LANES), F32),
                pltpu.SemaphoreType.DMA((5,)),
            ],
            compiler_params=pltpu.CompilerParams(vmem_limit_bytes=16 * 1024 * 1024),
        )(*parts)
        return jnp.transpose(offs, (1, 0, 2)), met, cen

    return jax.shard_map(
        per_device,
        mesh=mesh,
        in_specs=(
            P(None, None, ("gx", "gy")),
            P(None, ("gx", "gy")),
            P(None, ("gx", "gy")),
            P(),
            P(),
            P(("gx", "gy"), None, None),
            P(("gx", "gy"), None, None),
            P(("gx", "gy"), None, None),
            P(("gx", "gy"), None),
        ),
        out_specs=(P(None, None, ("gx", "gy")), P(None, ("gx", "gy")), P(None, ("gx", "gy"))),
        check_vma=False,
    )
```
